256 devices in a mesh: wide: 32 (over x, z), narrow: 8 (over y, core).
Axes of the slice: x: 4, y: 4, z: 8, core: 2. Of those that a mesh axis runs over, the one named last changes fastest.
Arguments:
- tokens: bfloat16 [1024, 8192], P('wide', 'narrow'), may hold values from -6 to 6
- gate_matrix: bfloat16 [8192, 28672], P('narrow', 'wide'), may hold values from -0.0625 to 0.0625
- up_matrix: bfloat16 [8192, 28672], P('narrow', 'wide'), may hold values from -0.0625 to 0.0625
- down_matrix: bfloat16 [28672, 8192], P('wide', 'narrow'), may hold values from -0.03125 to 0.03125
- adapter_down_factors: bfloat16 [8192, 256, 64], P('narrow', 'wide'), may hold values from -0.0625 to 0.0625
- adapter_up_factors: bfloat16 [256, 64, 28672], P('narrow', None, 'wide'), may hold values from -0.75 to 0.75
- adapter_index_rows: int32 [1024], replicated, may hold values from 0 to 255
Outputs:
- mixed: bfloat16 [1024, 8192], P('wide', 'narrow')
The draws below stay inside these ranges and needn't reach their ends.
All inputs are finite; a program needn't handle non-finite values.
Results may differ from the reference program's by a relative error of at most 0.0054.
Values may be sent and summed in bfloat16 or wider, within the bound.
No kernel may reach another device: no remote copies, remote signals or barrier semaphores. Data moves between devices by JAX's collectives and lax.ppermute only.
A program may use at most 128 MiB of HBM per device.

```python
import math
import jax
import jax.numpy as jnp
import numpy as np
from jax import lax

MODEL_WIDTH = 8192
HIDDEN_UNITS = 28672
ADAPTER_RANK = 64
REQUESTS = 1024
ADAPTER_COUNT = 256


def with_ends(array, stream_key, low, top_value):
    longest = array.shape.index(max(array.shape))
    spots = []
    for shift in (0, 1):
        where = [jax.random.randint(jax.random.fold_in(stream_key, axis), (), 0, length) for axis, length in enumerate(array.shape)]
        where[longest] = (where[longest] + shift) % array.shape[longest]
        spots.append(tuple(where))
    return array.at[spots[0]].set(low).at[spots[1]].set(top_value)


def shard_levels(key, dims, shards, low, largest):
    gain = 1.0
    for dim, blocks in shards:
        steps = jax.random.uniform(jax.random.fold_in(jax.random.fold_in(key, 6), dim), (blocks,), jnp.float32, low / len(shards), largest / len(shards))
        gain = gain * jnp.repeat(jnp.exp(steps), dims[dim] // blocks).reshape((-1,) + (1,) * (len(dims) - 1 - dim))
    return gain


def rank_bounds(count, skew):
    portions = [(1 << 20) // math.isqrt(grade ** skew) + 1 for grade in range(1, count + 1)]
    scale = 1 + sum(portions) // (1 << 30)
    return np.cumsum(np.array([max(1, weight // scale) for weight in portions]))


def skewed_ids(rng, shape, number_of, slope):
    listing = rank_bounds(number_of, slope)
    ticket = jax.random.randint(jax.random.fold_in(rng, 1), shape, 0, int(listing[number_of - 1]))
    rank = jnp.searchsorted(jnp.asarray(listing, jnp.int32), ticket, side="right")
    return jax.random.permutation(jax.random.fold_in(rng, 2), number_of)[rank].astype(jnp.int32)


def centred(stream_key, dims, deviation, bound, cuts=(), held_as=jnp.bfloat16):
    entries = deviation * jax.random.normal(stream_key, dims, jnp.float32)
    if cuts:
        entries = entries * shard_levels(stream_key, dims, cuts, -0.22, 0.18)
    return jnp.clip(entries, -bound, bound).astype(held_as)


def setup_inputs(seed: int = 0) -> dict:
    key_of = jax.random.split(jax.random.key(seed), 8)
    tokens = centred(key_of[0], (REQUESTS, MODEL_WIDTH), 1.0, 6.0, ((0, 32), (1, 8)))
    gate_matrix = centred(key_of[1], (MODEL_WIDTH, HIDDEN_UNITS), MODEL_WIDTH ** -0.5, 0.0625, ((0, 8), (1, 32)))
    up_matrix = centred(key_of[2], (MODEL_WIDTH, HIDDEN_UNITS), MODEL_WIDTH ** -0.5, 0.0625, ((0, 8), (1, 32)))
    down_matrix = centred(key_of[3], (HIDDEN_UNITS, MODEL_WIDTH), HIDDEN_UNITS ** -0.5, 0.03125, ((0, 32), (1, 8)))
    adapter_down_factors = centred(key_of[4], (MODEL_WIDTH, ADAPTER_COUNT, ADAPTER_RANK), MODEL_WIDTH ** -0.5, 0.0625, ((0, 8), (1, 32)))
    adapter_up_factors = centred(key_of[5], (ADAPTER_COUNT, ADAPTER_RANK, HIDDEN_UNITS), ADAPTER_RANK ** -0.5, 0.75, ((0, 8), (2, 32)))
    adapter_index_rows = with_ends(skewed_ids(key_of[6], (REQUESTS,), ADAPTER_COUNT, 2), jax.random.fold_in(key_of[6], 3), 0, ADAPTER_COUNT - 1).astype(jnp.int32)
    return {"tokens": tokens, "gate_matrix": gate_matrix, "up_matrix": up_matrix, "down_matrix": down_matrix, "adapter_down_factors": adapter_down_factors, "adapter_up_factors": adapter_up_factors, "adapter_index_rows": adapter_index_rows}


def reference(tokens, gate_matrix, up_matrix, down_matrix, adapter_down_factors, adapter_up_factors, adapter_index_rows):
    gate = jnp.dot(tokens, gate_matrix, preferred_element_type=jnp.float32)
    up = jnp.dot(tokens, up_matrix, preferred_element_type=jnp.float32)
    count = tokens.shape[0] // 16

    def one_block(items):
        rows, request_adapter_index = items
        lower_factor = jnp.take(adapter_down_factors, request_adapter_index, axis=1).astype(jnp.float32)
        low = jnp.einsum("rd,drk->rk", rows.astype(jnp.float32), lower_factor).astype(jnp.bfloat16)
        upper_factor = jnp.take(adapter_up_factors, request_adapter_index, axis=0).astype(jnp.float32)
        return jnp.einsum("rk,rkf->rf", low.astype(jnp.float32), upper_factor)

    delta = lax.map(one_block, (tokens.reshape(count, 16, tokens.shape[1]), adapter_index_rows.reshape(count, 16)))
    up = up + delta.reshape(tokens.shape[0], up.shape[1])
    hidden = (jax.nn.silu(gate) * up).astype(jnp.bfloat16)
    return jnp.dot(hidden, down_matrix, preferred_element_type=jnp.float32).astype(jnp.bfloat16)
```

```python
import jax
import jax.numpy as jnp
from jax import lax
from jax.sharding import PartitionSpec as P

NX, NZ, NY, NC = 4, 8, 4, 2
F32, BF16 = jnp.float32, jnp.bfloat16


def x_shift(d):
    return [(x * NZ + z, (x + d) % NX * NZ + z) for x in range(NX) for z in range(NZ)]


def y_shift(d):
    return [(y * NC + c, (y + d) % NY * NC + c) for y in range(NY) for c in range(NC)]


def home_move(k):
    return [
        ((x * NZ + z) * 8 + y * NC + c, ((y + k) % NY * NZ + z) * 8 + x * NC + c)
        for x in range(NX)
        for z in range(NZ)
        for y in range(NY)
        for c in range(NC)
    ]


Z_GROUPS = [[x * NZ + z for z in range(NZ)] for x in range(NX)]
CORE_SWAP = [(i, i ^ 1) for i in range(NY * NC)]


def core(v):
    return lax.ppermute(v, "narrow", CORE_SWAP)


def block(v, i):
    return lax.dynamic_index_in_dim(v, i, 0, keepdims=False)


def roll(v, by):
    return lax.dynamic_slice_in_dim(jnp.concatenate([v, v], 0), by, v.shape[0], 0)


def dot(a, b):
    return jnp.dot(a, b, preferred_element_type=F32)


def body(tokens, gate, up, down, a, b, index):
    w, n = lax.axis_index("wide"), lax.axis_index("narrow")
    x, y, c = w // NZ, n // NC, n % NC
    width, hid = gate.shape
    rank = a.shape[2]
    own_a, own_b = a.shape[1], b.shape[0]
    half = tokens.shape[0] // 2
    rows = NZ * half

    near = lax.dynamic_slice_in_dim(tokens, c * half, half, 0)
    far = core(lax.dynamic_slice_in_dim(tokens, (1 - c) * half, half, 0))
    gate_s, up_s, b_s, down_s = core(gate), core(up), core(b), core(down)
    a2 = a.reshape(width, own_a * rank)
    a_s = core(a2)

    shard = jnp.concatenate([near, far], 1)
    t0 = lax.all_to_all(
        jnp.broadcast_to(shard, (NZ,) + shard.shape), "wide", 0, 0, tiled=True, axis_index_groups=Z_GROUPS
    ).reshape(rows, 2 * width)
    t = jnp.concatenate([t0] + [lax.ppermute(t0, "wide", x_shift(-d)) for d in (1, 2, 3)], 0)
    t_n, t_f = t[:, :width], t[:, width:]

    index_rel = roll(block(index.reshape(NX, NZ, 2, half).transpose(2, 0, 1, 3), c).reshape(NX, rows), x)
    flat = index_rel.reshape(NX * rows)

    shrink = (dot(t_n, a2) + dot(t_f, a_s)).reshape(NX * rows, own_a, rank)
    pick = (flat[:, None] == w * own_a + jnp.arange(own_a, dtype=jnp.int32)[None]).astype(F32)
    low_part = jnp.sum(shrink * pick[:, :, None], 1).reshape(NX, rows, rank)
    low = 0.0
    for k in range(NY):
        low = low + lax.ppermute(block(low_part, (y + k - x) % NX), ("wide", "narrow"), home_move(k))
    low = low.astype(BF16)
    low = lax.all_to_all(
        jnp.broadcast_to(low, (NX * NZ,) + low.shape), "wide", 0, 0, tiled=True
    ).reshape(NX, NZ, rows, rank)
    low = roll(jnp.sum(low.astype(F32), 1).astype(BF16), x).reshape(NX * rows, rank)

    def reduce_y(part):
        part = part.reshape(NY, rows, hid)
        total = block(part, y)
        for d in (1, 2, 3):
            total = total + lax.ppermute(block(part, (y + d) % NY).astype(BF16), "narrow", y_shift(d)).astype(F32)
        return total

    gate_sum = reduce_y(dot(t_n, gate) + dot(t_f, gate_s))
    up_part = dot(t_n, up) + dot(t_f, up_s)
    for home, table in ((n, b), (n ^ 1, b_s)):
        mask = (flat[:, None] == home * own_b + jnp.arange(own_b, dtype=jnp.int32)[None]).astype(BF16)
        spread = (mask[:, :, None] * low[:, None, :]).reshape(NX * rows, own_b * rank)
        up_part = up_part + dot(spread, table.reshape(own_b * rank, hid))
    up_sum = reduce_y(up_part)
    hidden = (jax.nn.silu(gate_sum) * up_sum).astype(BF16)

    parts = jnp.stack([hidden] + [lax.ppermute(hidden, "narrow", y_shift(-d)) for d in (1, 2, 3)])
    h = roll(parts, (NY - y) % NY).reshape(NX * rows, hid)
    mixed = jnp.concatenate([dot(h, down), dot(h, down_s)], 1).reshape(NX, rows, 2 * width)
    total = mixed[0]
    for d in (1, 2, 3):
        total = total + lax.ppermute(mixed[d].astype(BF16), "wide", x_shift(d)).astype(F32)
    total = lax.all_to_all(
        total.astype(BF16).reshape(NZ, half, 2 * width), "wide", 0, 0, tiled=True, axis_index_groups=Z_GROUPS
    )
    total = jnp.sum(total.astype(F32), 0).astype(BF16)
    mine, other = total[:, :width], core(total[:, width:])
    return jnp.where(c == 0, jnp.concatenate([mine, other], 0), jnp.concatenate([other, mine], 0))


def solution(mesh):
    placed = (
        P("wide", "narrow"),
        P("narrow", "wide"),
        P("narrow", "wide"),
        P("wide", "narrow"),
        P("narrow", "wide", None),
        P("narrow", None, "wide"),
        P(),
    )
    return jax.shard_map(body, mesh=mesh, in_specs=placed, out_specs=P("wide", "narrow"), check_vma=False)
```

```python
import functools

import jax
import jax.numpy as jnp
from jax import lax
from jax.experimental import pallas as pl
from jax.experimental.pallas import tpu as pltpu
from jax.sharding import PartitionSpec as P

NX, NZ, NY, NC = 4, 8, 4, 2
F32, BF16 = jnp.float32, jnp.bfloat16
VMEM_LIMIT = 60 * 1024 * 1024


def device(x, z, y, c):
    return (x % NX * NZ + z % NZ) * NY * NC + y % NY * NC + c


def send_x(v, d):
    return lax.ppermute(v, "wide", [(x * NZ + z, (x + d) % NX * NZ + z) for x in range(NX) for z in range(NZ)])


def send_z(v, d):
    return lax.ppermute(v, "wide", [(x * NZ + z, x * NZ + (z + d) % NZ) for x in range(NX) for z in range(NZ)])


def send_y(v, d):
    return lax.ppermute(v, "narrow", [(y * NC + c, (y + d) % NY * NC + c) for y in range(NY) for c in range(NC)])


def send_pair(v):
    return lax.ppermute(v, "wide", [(i, i ^ 1) for i in range(NX * NZ)])


def send_home(v):
    cells = [(x, z, y, c) for x in range(NX) for z in range(NZ) for y in range(NY) for c in range(NC)]
    moves = [(device(x, z, y, c), device(y, z, x, c)) for x, z, y, c in cells]
    return lax.ppermute(v, ("wide", "narrow"), moves)


def core(v):
    return lax.ppermute(v, "narrow", [(i, i ^ 1) for i in range(NY * NC)])


Y_GROUPS = [[y * NC + c for y in range(NY)] for c in range(NC)]


def dot(a, b):
    return jnp.dot(a, b, preferred_element_type=F32)


SMEM = pl.BlockSpec(memory_space=pltpu.SMEM)
VMEM = pl.BlockSpec(memory_space=pltpu.VMEM)


def params():
    return pltpu.CompilerParams(vmem_limit_bytes=VMEM_LIMIT)


def together(*v):
    return lax.optimization_barrier(v)


def pick_kernel(place, q0, q1, q2, q3, keep, give):
    c = place[3]
    half = q0.shape[0] // 2
    for k, ref in enumerate((q0, q1, q2, q3)):
        at = slice(k * half, (k + 1) * half)
        keep[at, :] = ref[pl.ds(pl.multiple_of(c * half, half), half), :]
        give[at, :] = ref[pl.ds(pl.multiple_of((1 - c) * half, half), half), :]


def shrink_kernel(own, rank, place, index, p0, p1, p2, p3, q0, q1, a_n, a_f, t, low):
    x, z, first = place[0], place[1], place[4]
    half = t.shape[0] // (NX * NZ)
    width = a_n.shape[0]
    quads = NZ // 2

    def put(ref, at, dx, pair, k, columns):
        from_z = ((z ^ pair) + 2 * k) % NZ
        row = pl.multiple_of(((x + dx) % NX * NZ + from_z) * half, half)
        t[pl.ds(row, half), columns] = ref[at * half : (at + 1) * half, :]

    for dx, ref in enumerate((p0, p1, p2, p3)):
        for pair in range(2):
            for k in range(quads):
                put(ref, pair * quads + k, dx, pair, k, slice(0, width))
    for pair, ref in enumerate((q0, q1)):
        for dx in range(NX):
            for k in range(quads):
                put(ref, dx * quads + k, dx, pair, k, slice(width, 2 * width))
    s = dot(t[:, :width], a_n[...]) + dot(t[:, width:], a_f[...])
    total = jnp.zeros((t.shape[0], rank), F32)
    for k in range(own):
        total = jnp.where(index[...] == first + k, s[:, k * rank : (k + 1) * rank], total)
    total = total.reshape(NX, NZ * half, rank)
    some = NZ * half // 2
    low[...] = jnp.concatenate([total[:, :some], total[:, some:]], 2)


def gate_kernel(place, t, w_n, w_f, mine, o1, o2, o3):
    y = place[2]
    rows, width = mine.shape[0], w_n.shape[0]
    for e, ref in enumerate((mine, o1, o2, o3)):
        at = pl.ds(pl.multiple_of((y + e) % NY * rows, rows), rows)
        part = dot(t[at, :width], w_n[...]) + dot(t[at, width:], w_f[...])
        ref[...] = part.astype(ref.dtype)


def base_kernel(t, w_n, w_f, up):
    width = w_n.shape[0]
    up[...] = dot(t[:, :width], w_n[...]) + dot(t[:, width:], w_f[...])


def up_kernel(rank, place, index, low, up, b_n, b_f, mine, o1, o2, o3, total, wide_low):
    k, y = pl.program_id(0), place[2]
    step = b_n.shape[0]
    count = step // rank
    rows = mine.shape[0]

    @pl.when(k == 0)
    def _():
        v = jnp.sum(low[...].astype(F32).reshape(NX, NZ, rows // 2, 2 * rank), 1)
        v = jnp.concatenate([v[:, :, :rank], v[:, :, rank:]], 1).reshape(NX * rows, rank)
        wide_low[...] = jnp.concatenate([v] * count, 1)
        total[...] = up[...]

    group = (lax.broadcasted_iota(jnp.int32, (NX * rows, step), 1) >> (rank.bit_length() - 1)) + k * count
    own = index[...] - place[5]
    far = index[...] - place[6]
    spread_n = jnp.where(own == group, wide_low[...], 0.0).astype(BF16)
    spread_f = jnp.where(far == group, wide_low[...], 0.0).astype(BF16)
    total[...] += dot(spread_n, b_n[...]) + dot(spread_f, b_f[...])

    @pl.when(k == pl.num_programs(0) - 1)
    def _():
        for e, ref in enumerate((mine, o1, o2, o3)):
            at = pl.ds(pl.multiple_of((y + e) % NY * rows, rows), rows)
            ref[...] = total[at, :].astype(ref.dtype)


def mix_kernel(place, h0, h1, h2, h3, d_n, d_f, near0, near1, near2, near3, far0, far1, h):
    x, z, y = place[0], place[1], place[2]
    half = h0.shape[0] // NZ
    quads = NZ // 2
    for e, ref in enumerate((h0, h1, h2, h3)):
        dx = (y + e - x + NX) % NX
        for pair in range(2):
            for k in range(quads):
                to_z = ((z ^ pair) + 2 * k) % NZ
                to = pl.multiple_of(((dx * 2 + pair) * quads + k) * half, half)
                h[pl.ds(to, half), :] = ref[pl.ds(pl.multiple_of(to_z * half, half), half), :]
    rows = NZ * half
    near = dot(h[...], d_n[...])
    for dx, ref in enumerate((near0, near1, near2, near3)):
        ref[...] = near[dx * rows : (dx + 1) * rows].astype(ref.dtype)
    far = dot(h[...], d_f[...])
    some = rows // 2
    for dx in range(NX):
        for pair, ref in enumerate((far0, far1)):
            at = (dx * 2 + pair) * some
            ref[dx * some : (dx + 1) * some, :] = far[at : at + some].astype(ref.dtype)


def body(tokens, gate, up, down, a, b, index):
    w, n = lax.axis_index("wide"), lax.axis_index("narrow")
    x, z, y, c = w // NZ, w % NZ, n // NC, n % NC
    width, hid = gate.shape
    own_a, rank, own_b = a.shape[1], a.shape[2], b.shape[0]
    half = tokens.shape[0] // 2
    rows = NZ * half
    everyone = NX * rows
    shape = jax.ShapeDtypeStruct

    a_n = a.reshape(width, own_a * rank)
    b_n = b.reshape(own_b * rank, hid)
    place = jnp.stack([x, z, y, c, w * own_a, n * own_b, (n ^ 1) * own_b]).astype(jnp.int32)
    column = lax.dynamic_index_in_dim(index.reshape(NX * NZ, 2, half), c, 1, keepdims=False).reshape(everyone, 1)

    *quad, b_f, gate_f, place, column = together(
        *[send_z(tokens, -2 * k) for k in (1, 2, 3)], core(b_n), core(gate), place, column
    )
    near, far = pl.pallas_call(
        pick_kernel,
        out_shape=(shape((rows // 2, width), BF16),) * 2,
        in_specs=[SMEM] + [VMEM] * 4,
        out_specs=(VMEM,) * 2,
        compiler_params=params(),
        name="pick",
    )(place, tokens, *quad)
    a_n, far, near = together(a_n, far, near)
    far, a_f, up = together(core(far), core(a_n), up)
    pair, *fars, up_f = together(send_pair(near), *[send_x(far, -d) for d in (1, 2, 3)], core(up))
    down, near, pair = together(down, near, pair)
    near = jnp.concatenate([near, pair], 0)
    far = jnp.concatenate([far] + fars, 0)
    *pieces, down_f = together(near, *[send_x(near, -d) for d in (1, 2, 3)], far, send_pair(far), core(down))
    t, low = pl.pallas_call(
        functools.partial(shrink_kernel, own_a, rank),
        out_shape=(shape((everyone, 2 * width), BF16),) + (shape((NX, rows // 2, 2 * rank), F32),),
        in_specs=[SMEM] + [VMEM] * 9,
        out_specs=(VMEM,) * 2,
        compiler_params=params(),
        name="shrink",
    )(place, column, *pieces, a_n, a_f)

    blocks = (shape((rows, hid), F32),) + (shape((rows, hid), BF16),) * 3

    def reduce_y(mine, *others):
        for e, part in enumerate(others, 1):
            mine = mine + send_y(part, e).astype(F32)
        return mine

    gates = pl.pallas_call(
        gate_kernel,
        out_shape=blocks,
        in_specs=[SMEM] + [VMEM] * 3,
        out_specs=(VMEM,) * 4,
        compiler_params=params(),
        name="gate",
    )(place, t, gate, gate_f)

    low, *gates = together(
        lax.all_to_all(low, "narrow", 0, 0, tiled=True, axis_index_groups=Y_GROUPS), *gates
    )
    low, t, *gates = together(send_home(jnp.sum(low, 0).astype(BF16)), t, *gates)
    low = lax.all_to_all(jnp.broadcast_to(low, (NX * NZ,) + low.shape), "wide", 0, 0, tiled=True)

    up_part = pl.pallas_call(
        base_kernel,
        out_shape=shape((everyone, hid), F32),
        in_specs=[VMEM] * 3,
        out_specs=VMEM,
        compiler_params=params(),
        name="base",
    )(t, up, up_f)
    gate_sum = reduce_y(*gates)
    steps = 4
    part = pl.BlockSpec((own_b * rank // steps, hid), lambda k: (k, 0))
    fixed = lambda *dims: pl.BlockSpec(dims, lambda k: (0,) * len(dims))
    up_sum = reduce_y(
        *pl.pallas_call(
            functools.partial(up_kernel, rank),
            out_shape=blocks,
            grid=(steps,),
            in_specs=[SMEM, fixed(everyone, 1), fixed(*low.shape), fixed(everyone, hid), part, part],
            out_specs=(fixed(rows, hid),) * 4,
            scratch_shapes=[pltpu.VMEM((everyone, hid), F32), pltpu.VMEM((everyone, own_b * rank // steps), F32)],
            compiler_params=params(),
            name="up",
        )(place, column, low, up_part, b_n, b_f)
    )
    hidden = (jax.nn.silu(gate_sum) * up_sum).astype(BF16)

    some = everyone // 2
    near, n1, n2, n3, far, f1 = pl.pallas_call(
        mix_kernel,
        out_shape=(shape((rows, width), F32),)
        + (shape((rows, width), BF16),) * 3
        + (shape((some, width), F32), shape((some, width), BF16)),
        in_specs=[SMEM] + [VMEM] * 6,
        out_specs=(VMEM,) * 6,
        scratch_shapes=[pltpu.VMEM((everyone, hid), BF16)],
        compiler_params=params(),
        name="mix",
    )(place, hidden, *[send_y(hidden, -e) for e in (1, 2, 3)], down, down_f)
    n1, n2, n3, f1 = together(send_x(n1, 1), send_x(n2, 2), send_x(n3, 3), send_pair(f1))
    near = near + n1.astype(F32) + n2.astype(F32) + n3.astype(F32)
    far = (far + f1.astype(F32)).reshape(NX, rows // 2, width)
    n1, f1, f2, f3 = together(
        send_pair(near[rows // 2 :].astype(BF16)), *[send_x(far[d].astype(BF16), d) for d in (1, 2, 3)]
    )
    near = near[: rows // 2] + n1.astype(F32)
    far = far[0] + f1.astype(F32) + f2.astype(F32) + f3.astype(F32)
    both = jnp.concatenate([near, far], 1).reshape(NZ // 2, half, 2 * width)
    total = both[0]
    for v in together(*[send_z(both[k].astype(BF16), 2 * k) for k in (1, 2, 3)]):
        total = total + v.astype(F32)
    total = total.astype(BF16)
    mine, other = total[:, :width], core(total[:, width:])
    return jnp.where(c == 0, jnp.concatenate([mine, other], 0), jnp.concatenate([other, mine], 0))


def solution(mesh):
    placed = (
        P("wide", "narrow"),
        P("narrow", "wide"),
        P("narrow", "wide"),
        P("wide", "narrow"),
        P("narrow", "wide", None),
        P("narrow", None, "wide"),
        P(),
    )
    return jax.shard_map(body, mesh=mesh, in_specs=placed, out_specs=P("wide", "narrow"), check_vma=False)
```

```python
import functools

import jax
import jax.numpy as jnp
from jax import lax
from jax.experimental import pallas as pl
from jax.experimental.pallas import tpu as pltpu
from jax.sharding import PartitionSpec as P

NX, NZ, NY, NC = 4, 8, 4, 2
F32, BF16 = jnp.float32, jnp.bfloat16
MIB = 1024 * 1024


def device(x, z, y, c):
    return (x % NX * NZ + z % NZ) * NY * NC + y % NY * NC + c


def send_x(v, d):
    return lax.ppermute(v, "wide", [(x * NZ + z, (x + d) % NX * NZ + z) for x in range(NX) for z in range(NZ)])


def send_z(v, d):
    return lax.ppermute(v, "wide", [(x * NZ + z, x * NZ + (z + d) % NZ) for x in range(NX) for z in range(NZ)])


def send_y(v, d):
    return lax.ppermute(v, "narrow", [(y * NC + c, (y + d) % NY * NC + c) for y in range(NY) for c in range(NC)])


def send_pair(v):
    return lax.ppermute(v, "wide", [(i, i ^ 1) for i in range(NX * NZ)])


def core(v):
    return lax.ppermute(v, "narrow", [(i, i ^ 1) for i in range(NY * NC)])


HOME_GROUPS = [
    [device(x, z + p, y, c) for x in range(NX) for y in range(NY) for p in range(2)]
    for z in range(0, NZ, 2)
    for c in range(NC)
]


def dot(a, b):
    return jnp.dot(a, b, preferred_element_type=F32)


SMEM = pl.BlockSpec(memory_space=pltpu.SMEM)
VMEM = pl.BlockSpec(memory_space=pltpu.VMEM)


def params(limit=60 * MIB):
    return pltpu.CompilerParams(vmem_limit_bytes=limit)


def together(*v):
    return lax.optimization_barrier(v)


def pick_kernel(place, q0, q1, q2, q3, keep, give):
    c = place[3]
    half = q0.shape[0] // 2
    for k, ref in enumerate((q0, q1, q2, q3)):
        at = slice(k * half, (k + 1) * half)
        keep[at, :] = ref[pl.ds(pl.multiple_of(c * half, half), half), :]
        give[at, :] = ref[pl.ds(pl.multiple_of((1 - c) * half, half), half), :]


def join_kernel(n0, n1, f0, f1, f2, f3, near, far):
    some = n0.shape[0]
    for k, ref in enumerate((n0, n1)):
        near[k * some : (k + 1) * some, :] = ref[...]
    for k, ref in enumerate((f0, f1, f2, f3)):
        far[k * some : (k + 1) * some, :] = ref[...]


def shrink_kernel(own, rank, place, index, p0, p1, p2, p3, q0, q1, a_n, a_f, t, low):
    x, z, first = place[0], place[1], place[4]
    half = t.shape[0] // (NX * NZ)
    width = a_n.shape[0]
    quads = NZ // 2

    def put(ref, at, dx, pair, k, columns):
        from_z = ((z ^ pair) + 2 * k) % NZ
        row = pl.multiple_of(((x + dx) % NX * NZ + from_z) * half, half)
        t[pl.ds(row, half), columns] = ref[at * half : (at + 1) * half, :]

    for dx, ref in enumerate((p0, p1, p2, p3)):
        for pair in range(2):
            for k in range(quads):
                put(ref, pair * quads + k, dx, pair, k, slice(0, width))
    for pair, ref in enumerate((q0, q1)):
        for dx in range(NX):
            for k in range(quads):
                put(ref, dx * quads + k, dx, pair, k, slice(width, 2 * width))
    s = dot(t[:, :width], a_n[...]) + dot(t[:, width:], a_f[...])
    total = jnp.zeros((t.shape[0], rank), F32)
    for k in range(own):
        total = jnp.where(index[...] == first + k, s[:, k * rank : (k + 1) * rank], total)
    some = NZ * half // 4
    total = total.reshape(NX, 2, 2 * some, rank)
    total = jnp.concatenate([total[:, :, :some], total[:, :, some:]], 3)
    for b in range(NX):
        for y in range(NY):
            for p in range(2):
                low[(b * NY + y) * 2 + p] = total[b, p]


def gate_kernel(place, t, w_n, w_f, mine, o1, o2, o3):
    y = place[2]
    rows, width = mine.shape[0], w_n.shape[0]
    for e, ref in enumerate((mine, o1, o2, o3)):
        at = pl.ds(pl.multiple_of((y + e) % NY * rows, rows), rows)
        part = dot(t[at, :width], w_n[...]) + dot(t[at, width:], w_f[...])
        ref[...] = part.astype(ref.dtype)


def base_kernel(t, w_n, w_f, up):
    width = w_n.shape[0]
    up[...] = dot(t[:, :width], w_n[...]) + dot(t[:, width:], w_f[...])


def up_kernel(rank, place, index, low, up, b_n, b_f, mine, o1, o2, o3, total, wide_low):
    k, y = pl.program_id(0), place[2]
    step = b_n.shape[0]
    count = step // rank
    rows = mine.shape[0]

    @pl.when(k == 0)
    def _():
        v = jnp.sum(low[...].astype(F32).reshape(NX, NZ // 2, 2, rows // 4, 2 * rank), 1)
        v = jnp.concatenate([v[:, :, :, :rank], v[:, :, :, rank:]], 2).reshape(NX * rows, rank)
        wide_low[...] = jnp.concatenate([v] * count, 1)
        total[...] = up[...]

    group = (lax.broadcasted_iota(jnp.int32, (NX * rows, step), 1) >> (rank.bit_length() - 1)) + k * count
    own = index[...] - place[5]
    far = index[...] - place[6]
    spread_n = jnp.where(own == group, wide_low[...], 0.0).astype(BF16)
    spread_f = jnp.where(far == group, wide_low[...], 0.0).astype(BF16)
    total[...] += dot(spread_n, b_n[...]) + dot(spread_f, b_f[...])

    @pl.when(k == pl.num_programs(0) - 1)
    def _():
        for e, ref in enumerate((mine, o1, o2, o3)):
            at = pl.ds(pl.multiple_of((y + e) % NY * rows, rows), rows)
            ref[...] = total[at, :].astype(ref.dtype)


def mix_kernel(place, h0, h1, h2, h3, d_n, d_f, near0, near1, near2, near3, far0, far1, h):
    x, z, y = place[0], place[1], place[2]
    half = h0.shape[0] // NZ
    quads = NZ // 2
    for e, ref in enumerate((h0, h1, h2, h3)):
        dx = (y + e - x + NX) % NX
        for pair in range(2):
            for k in range(quads):
                to_z = ((z ^ pair) + 2 * k) % NZ
                to = pl.multiple_of(((dx * 2 + pair) * quads + k) * half, half)
                h[pl.ds(to, half), :] = ref[pl.ds(pl.multiple_of(to_z * half, half), half), :]
    rows = NZ * half
    near = dot(h[...], d_n[...])
    for dx, ref in enumerate((near0, near1, near2, near3)):
        ref[...] = near[dx * rows : (dx + 1) * rows].astype(ref.dtype)
    far = dot(h[...], d_f[...])
    some = rows // 2
    for dx in range(NX):
        for pair, ref in enumerate((far0, far1)):
            at = (dx * 2 + pair) * some
            ref[dx * some : (dx + 1) * some, :] = far[at : at + some].astype(ref.dtype)


def body(tokens, gate, up, down, a, b, index):
    w, n = lax.axis_index("wide"), lax.axis_index("narrow")
    x, z, y, c = w // NZ, w % NZ, n // NC, n % NC
    width, hid = gate.shape
    own_a, rank, own_b = a.shape[1], a.shape[2], b.shape[0]
    half = tokens.shape[0] // 2
    rows = NZ * half
    everyone = NX * rows
    shape = jax.ShapeDtypeStruct

    b_n = b.reshape(own_b * rank, hid)
    place = jnp.stack([x, z, y, c, w * own_a, n * own_b, (n ^ 1) * own_b]).astype(jnp.int32)
    column = lax.dynamic_index_in_dim(index.reshape(NX * NZ, 2, half), c, 1, keepdims=False).reshape(everyone, 1)

    *quad, b_f, gate_f, place, column = together(
        *[send_z(tokens, -2 * k) for k in (1, 2, 3)], core(b_n), core(gate), place, column
    )
    near, far = pl.pallas_call(
        pick_kernel,
        out_shape=(shape((rows // 2, width), BF16),) * 2,
        in_specs=[SMEM] + [VMEM] * 4,
        out_specs=(VMEM,) * 2,
        compiler_params=params(4 * MIB),
        name="pick",
    )(place, tokens, *quad)
    far, up = together(core(far), up)
    a_n = a.reshape(width, own_a * rank)
    pair, *fars, a_f = together(send_pair(near), *[send_x(far, -d) for d in (1, 2, 3)], core(a_n))
    near, far = pl.pallas_call(
        join_kernel,
        out_shape=(shape((rows, width), BF16), shape((everyone // 2, width), BF16)),
        in_specs=[VMEM] * 6,
        out_specs=(VMEM,) * 2,
        compiler_params=params(4 * MIB),
        name="join",
    )(near, pair, far, *fars)
    *pieces, up_f = together(near, *[send_x(near, -d) for d in (1, 2, 3)], far, send_pair(far), core(up))
    down, gate = together(down, gate, up_f)[:2]
    down_f = core(down)
    t, low = pl.pallas_call(
        functools.partial(shrink_kernel, own_a, rank),
        out_shape=(shape((everyone, 2 * width), BF16),) + (shape((2 * NX * NY, rows // 4, 2 * rank), F32),),
        in_specs=[SMEM] + [VMEM] * 9,
        out_specs=(VMEM,) * 2,
        compiler_params=params(),
        name="shrink",
    )(place, column, *pieces, a_n, a_f)

    blocks = (shape((rows, hid), F32),) + (shape((rows, hid), BF16),) * 3

    def reduce_y(mine, *others):
        for e, part in enumerate(others, 1):
            mine = mine + send_y(part, e).astype(F32)
        return mine

    gates = pl.pallas_call(
        gate_kernel,
        out_shape=blocks,
        in_specs=[SMEM] + [VMEM] * 3,
        out_specs=(VMEM,) * 4,
        compiler_params=params(),
        name="gate",
    )(place, t, gate, gate_f)

    low, t, *gates = together(
        lax.all_to_all(low, ("wide", "narrow"), 0, 0, tiled=True, axis_index_groups=HOME_GROUPS), t, *gates
    )
    low = lax.dynamic_slice_in_dim(low, y * 2 * NY, 2 * NY, 0)
    low = jnp.sum(low, 0).astype(BF16)
    low = lax.all_to_all(jnp.broadcast_to(low, (NX * NZ,) + low.shape), "wide", 0, 0, tiled=True)

    up_part = pl.pallas_call(
        base_kernel,
        out_shape=shape((everyone, hid), F32),
        in_specs=[VMEM] * 3,
        out_specs=VMEM,
        compiler_params=params(),
        name="base",
    )(t, up, up_f)
    gate_sum = reduce_y(*gates)
    steps = 4
    part = pl.BlockSpec((own_b * rank // steps, hid), lambda k: (k, 0))
    fixed = lambda *dims: pl.BlockSpec(dims, lambda k: (0,) * len(dims))
    up_sum = reduce_y(
        *pl.pallas_call(
            functools.partial(up_kernel, rank),
            out_shape=blocks,
            grid=(steps,),
            in_specs=[SMEM, fixed(everyone, 1), fixed(*low.shape), fixed(everyone, hid), part, part],
            out_specs=(fixed(rows, hid),) * 4,
            scratch_shapes=[pltpu.VMEM((everyone, hid), F32), pltpu.VMEM((everyone, own_b * rank // steps), F32)],
            compiler_params=params(),
            name="up",
        )(place, column, low, up_part, b_n, b_f)
    )
    hidden = (jax.nn.silu(gate_sum) * up_sum).astype(BF16)

    some = everyone // 2
    near, n1, n2, n3, far, f1 = pl.pallas_call(
        mix_kernel,
        out_shape=(shape((rows, width), F32),)
        + (shape((rows, width), BF16),) * 3
        + (shape((some, width), F32), shape((some, width), BF16)),
        in_specs=[SMEM] + [VMEM] * 6,
        out_specs=(VMEM,) * 6,
        scratch_shapes=[pltpu.VMEM((everyone, hid), BF16)],
        compiler_params=params(24 * MIB),
        name="mix",
    )(place, hidden, *[send_y(hidden, -e) for e in (1, 2, 3)], down, down_f)
    n1, n2, n3, f1 = together(send_x(n1, 1), send_x(n2, 2), send_x(n3, 3), send_pair(f1))
    near = near + n1.astype(F32) + n2.astype(F32) + n3.astype(F32)
    far = (far + f1.astype(F32)).reshape(NX, rows // 2, width)
    n1, f1, f2, f3 = together(
        send_pair(near[rows // 2 :].astype(BF16)), *[send_x(far[d].astype(BF16), d) for d in (1, 2, 3)]
    )
    near = near[: rows // 2] + n1.astype(F32)
    far = far[0] + f1.astype(F32) + f2.astype(F32) + f3.astype(F32)
    both = jnp.concatenate([near, far], 1).reshape(NZ // 2, half, 2 * width)
    total = both[0]
    for v in together(*[send_z(both[k].astype(BF16), 2 * k) for k in (1, 2, 3)]):
        total = total + v.astype(F32)
    total = total.astype(BF16)
    mine, other = total[:, :width], core(total[:, width:])
    return jnp.where(c == 0, jnp.concatenate([mine, other], 0), jnp.concatenate([other, mine], 0))


def solution(mesh):
    placed = (
        P("wide", "narrow"),
        P("narrow", "wide"),
        P("narrow", "wide"),
        P("wide", "narrow"),
        P("narrow", "wide", None),
        P("narrow", None, "wide"),
        P(),
    )
    return jax.shard_map(body, mesh=mesh, in_specs=placed, out_specs=P("wide", "narrow"), check_vma=False)
```

```python
import functools

import jax
import jax.numpy as jnp
from jax import lax
from jax.experimental import pallas as pl
from jax.experimental.pallas import tpu as pltpu
from jax.sharding import PartitionSpec as P

NX, NZ, NY, NC = 4, 8, 4, 2
F32, BF16 = jnp.float32, jnp.bfloat16
MIB = 1024 * 1024


def device(x, z, y, c):
    return (x % NX * NZ + z % NZ) * NY * NC + y % NY * NC + c


def send_x(v, d):
    return lax.ppermute(v, "wide", [(x * NZ + z, (x + d) % NX * NZ + z) for x in range(NX) for z in range(NZ)])


def send_z(v, d):
    return lax.ppermute(v, "wide", [(x * NZ + z, x * NZ + (z + d) % NZ) for x in range(NX) for z in range(NZ)])


def send_y(v, d):
    return lax.ppermute(v, "narrow", [(y * NC + c, (y + d) % NY * NC + c) for y in range(NY) for c in range(NC)])


def send_pair(v):
    return lax.ppermute(v, "wide", [(i, i ^ 1) for i in range(NX * NZ)])


def core(v):
    return lax.ppermute(v, "narrow", [(i, i ^ 1) for i in range(NY * NC)])


HOME_GROUPS = [
    [device(x, z + p, y, c) for x in range(NX) for y in range(NY) for p in range(2)]
    for z in range(0, NZ, 2)
    for c in range(NC)
]


def dot(a, b):
    return jnp.dot(a, b, preferred_element_type=F32)


SMEM = pl.BlockSpec(memory_space=pltpu.SMEM)
VMEM = pl.BlockSpec(memory_space=pltpu.VMEM)


def params(limit=60 * MIB):
    return pltpu.CompilerParams(vmem_limit_bytes=limit)


def together(*v):
    return lax.optimization_barrier(v)


def in_hbm(*arrays):
    return [pltpu.with_memory_space_constraint(v, pltpu.HBM) for v in arrays]


def pick_kernel(place, q0, q1, q2, q3, keep, give):
    c = place[3]
    half = q0.shape[0] // 2
    for k, ref in enumerate((q0, q1, q2, q3)):
        at = slice(k * half, (k + 1) * half)
        keep[at, :] = ref[pl.ds(pl.multiple_of(c * half, half), half), :]
        give[at, :] = ref[pl.ds(pl.multiple_of((1 - c) * half, half), half), :]


def join_kernel(n0, n1, f0, f1, f2, f3, near, far):
    some = n0.shape[0]
    for k, ref in enumerate((n0, n1)):
        near[k * some : (k + 1) * some, :] = ref[...]
    for k, ref in enumerate((f0, f1, f2, f3)):
        far[k * some : (k + 1) * some, :] = ref[...]


def shrink_kernel(own, rank, place, index, p0, p1, p2, p3, q0, q1, a_n, a_f, t, low):
    x, z, first = place[0], place[1], place[4]
    half = t.shape[0] // (NX * NZ)
    width = a_n.shape[0]
    quads = NZ // 2

    def put(ref, at, dx, pair, k, columns):
        from_z = ((z ^ pair) + 2 * k) % NZ
        row = pl.multiple_of(((x + dx) % NX * NZ + from_z) * half, half)
        t[pl.ds(row, half), columns] = ref[at * half : (at + 1) * half, :]

    for dx, ref in enumerate((p0, p1, p2, p3)):
        for pair in range(2):
            for k in range(quads):
                put(ref, pair * quads + k, dx, pair, k, slice(0, width))
    for pair, ref in enumerate((q0, q1)):
        for dx in range(NX):
            for k in range(quads):
                put(ref, dx * quads + k, dx, pair, k, slice(width, 2 * width))
    s = dot(t[:, :width], a_n[...]) + dot(t[:, width:], a_f[...])
    total = jnp.zeros((t.shape[0], rank), F32)
    for k in range(own):
        total = jnp.where(index[...] == first + k, s[:, k * rank : (k + 1) * rank], total)
    some = NZ * half // 4
    total = total.reshape(NX, 2, 2 * some, rank)
    total = jnp.concatenate([total[:, :, :some], total[:, :, some:]], 3)
    for b in range(NX):
        for y in range(NY):
            for p in range(2):
                low[(b * NY + y) * 2 + p] = total[b, p]


def gate_kernel(place, t, w_n, w_f, mine, o1, o2, o3):
    y = place[2]
    rows, width = mine.shape[0], w_n.shape[0]
    for e, ref in enumerate((mine, o1, o2, o3)):
        at = pl.ds(pl.multiple_of((y + e) % NY * rows, rows), rows)
        part = dot(t[at, :width], w_n[...]) + dot(t[at, width:], w_f[...])
        ref[...] = part.astype(ref.dtype)


def base_kernel(t, w_n, w_f, up):
    width = w_n.shape[0]
    up[...] = dot(t[:, :width], w_n[...]) + dot(t[:, width:], w_f[...])


def up_kernel(rank, place, index, low, up, b_n, b_f, mine, o1, o2, o3, total, wide_low):
    k, y = pl.program_id(0), place[2]
    step = b_n.shape[0]
    count = step // rank
    rows = mine.shape[0]

    @pl.when(k == 0)
    def _():
        v = jnp.sum(low[...].astype(F32).reshape(NX, NZ // 2, 2, rows // 4, 2 * rank), 1)
        v = jnp.concatenate([v[:, :, :, :rank], v[:, :, :, rank:]], 2).reshape(NX * rows, rank)
        wide_low[...] = jnp.concatenate([v] * count, 1)
        total[...] = up[...]

    group = (lax.broadcasted_iota(jnp.int32, (NX * rows, step), 1) >> (rank.bit_length() - 1)) + k * count
    own = index[...] - place[5]
    far = index[...] - place[6]
    spread_n = jnp.where(own == group, wide_low[...], 0.0).astype(BF16)
    spread_f = jnp.where(far == group, wide_low[...], 0.0).astype(BF16)
    total[...] += dot(spread_n, b_n[...]) + dot(spread_f, b_f[...])

    @pl.when(k == pl.num_programs(0) - 1)
    def _():
        for e, ref in enumerate((mine, o1, o2, o3)):
            at = pl.ds(pl.multiple_of((y + e) % NY * rows, rows), rows)
            ref[...] = total[at, :].astype(ref.dtype)


def mix_kernel(place, h0, h1, h2, h3, d_n, d_f, near0, near1, near2, near3, far0, far1, h):
    x, z, y = place[0], place[1], place[2]
    half = h0.shape[0] // NZ
    quads = NZ // 2
    for e, ref in enumerate((h0, h1, h2, h3)):
        dx = (y + e - x + NX) % NX
        for pair in range(2):
            for k in range(quads):
                to_z = ((z ^ pair) + 2 * k) % NZ
                to = pl.multiple_of(((dx * 2 + pair) * quads + k) * half, half)
                h[pl.ds(to, half), :] = ref[pl.ds(pl.multiple_of(to_z * half, half), half), :]
    rows = NZ * half
    near = dot(h[...], d_n[...])
    for dx, ref in enumerate((near0, near1, near2, near3)):
        ref[...] = near[dx * rows : (dx + 1) * rows].astype(ref.dtype)
    far = dot(h[...], d_f[...])
    some = rows // 2
    for dx in range(NX):
        for pair, ref in enumerate((far0, far1)):
            at = (dx * 2 + pair) * some
            ref[dx * some : (dx + 1) * some, :] = far[at : at + some].astype(ref.dtype)


def body(tokens, gate, up, down, a, b, index):
    w, n = lax.axis_index("wide"), lax.axis_index("narrow")
    x, z, y, c = w // NZ, w % NZ, n // NC, n % NC
    width, hid = gate.shape
    own_a, rank, own_b = a.shape[1], a.shape[2], b.shape[0]
    half = tokens.shape[0] // 2
    rows = NZ * half
    everyone = NX * rows
    shape = jax.ShapeDtypeStruct

    b_n = b.reshape(own_b * rank, hid)
    place = jnp.stack([x, z, y, c, w * own_a, n * own_b, (n ^ 1) * own_b]).astype(jnp.int32)
    column = lax.dynamic_index_in_dim(index.reshape(NX * NZ, 2, half), c, 1, keepdims=False).reshape(everyone, 1)

    *quad, b_f, gate_f, place, column = together(
        *[send_z(tokens, -2 * k) for k in (1, 2, 3)], core(b_n), core(gate), place, column
    )
    near, far = pl.pallas_call(
        pick_kernel,
        out_shape=(shape((rows // 2, width), BF16),) * 2,
        in_specs=[SMEM] + [VMEM] * 4,
        out_specs=(VMEM,) * 2,
        compiler_params=params(4 * MIB),
        name="pick",
    )(place, *in_hbm(tokens), *quad)
    far, up = together(core(far), up)
    a_n = a.reshape(width, own_a * rank)
    pair, *fars, a_f = together(send_pair(near), *[send_x(far, -d) for d in (1, 2, 3)], core(a_n))
    near, far = pl.pallas_call(
        join_kernel,
        out_shape=(shape((rows, width), BF16), shape((everyone // 2, width), BF16)),
        in_specs=[VMEM] * 6,
        out_specs=(VMEM,) * 2,
        compiler_params=params(4 * MIB),
        name="join",
    )(near, pair, far, *fars)
    *pieces, up_f = together(near, *[send_x(near, -d) for d in (1, 2, 3)], far, send_pair(far), core(up))
    down, gate = together(down, gate, up_f)[:2]
    down_f = core(down)
    t, low = pl.pallas_call(
        functools.partial(shrink_kernel, own_a, rank),
        out_shape=(shape((everyone, 2 * width), BF16),) + (shape((2 * NX * NY, rows // 4, 2 * rank), F32),),
        in_specs=[SMEM] + [VMEM] * 9,
        out_specs=(VMEM,) * 2,
        compiler_params=params(),
        name="shrink",
    )(place, column, *pieces, a_n, a_f)

    blocks = (shape((rows, hid), F32),) + (shape((rows, hid), BF16),) * 3

    def reduce_y(mine, *others):
        for e, part in enumerate(others, 1):
            mine = mine + send_y(part, e).astype(F32)
        return mine

    gates = pl.pallas_call(
        gate_kernel,
        out_shape=blocks,
        in_specs=[SMEM] + [VMEM] * 3,
        out_specs=(VMEM,) * 4,
        compiler_params=params(),
        name="gate",
    )(place, t, gate, gate_f)

    low, t, *gates = together(
        lax.all_to_all(low, ("wide", "narrow"), 0, 0, tiled=True, axis_index_groups=HOME_GROUPS), t, *gates
    )
    low = lax.dynamic_slice_in_dim(low, y * 2 * NY, 2 * NY, 0)
    low = jnp.sum(low, 0).astype(BF16)
    low = lax.all_to_all(jnp.broadcast_to(low, (NX * NZ,) + low.shape), "wide", 0, 0, tiled=True)

    up_part = pl.pallas_call(
        base_kernel,
        out_shape=shape((everyone, hid), F32),
        in_specs=[VMEM] * 3,
        out_specs=VMEM,
        compiler_params=params(),
        name="base",
    )(t, up, up_f)
    gate_sum = reduce_y(*gates)
    steps = 4
    part = pl.BlockSpec((own_b * rank // steps, hid), lambda k: (k, 0))
    fixed = lambda *dims: pl.BlockSpec(dims, lambda k: (0,) * len(dims))
    up_sum = reduce_y(
        *pl.pallas_call(
            functools.partial(up_kernel, rank),
            out_shape=blocks,
            grid=(steps,),
            in_specs=[SMEM, fixed(everyone, 1), fixed(*low.shape), fixed(everyone, hid), part, part],
            out_specs=(fixed(rows, hid),) * 4,
            scratch_shapes=[pltpu.VMEM((everyone, hid), F32), pltpu.VMEM((everyone, own_b * rank // steps), F32)],
            compiler_params=params(32 * MIB),
            name="up",
        )(place, column, low, *in_hbm(up_part, b_n, b_f))
    )
    hidden = (jax.nn.silu(gate_sum) * up_sum).astype(BF16)

    some = everyone // 2
    near, n1, n2, n3, far, f1 = pl.pallas_call(
        mix_kernel,
        out_shape=(shape((rows, width), F32),)
        + (shape((rows, width), BF16),) * 3
        + (shape((some, width), F32), shape((some, width), BF16)),
        in_specs=[SMEM] + [VMEM] * 6,
        out_specs=(VMEM,) * 6,
        scratch_shapes=[pltpu.VMEM((everyone, hid), BF16)],
        compiler_params=params(24 * MIB),
        name="mix",
    )(place, hidden, *[send_y(hidden, -e) for e in (1, 2, 3)], down, down_f)
    n1, n2, n3, f1 = together(send_x(n1, 1), send_x(n2, 2), send_x(n3, 3), send_pair(f1))
    near = near + n1.astype(F32) + n2.astype(F32) + n3.astype(F32)
    far = (far + f1.astype(F32)).reshape(NX, rows // 2, width)
    n1, f1, f2, f3 = together(
        send_pair(near[rows // 2 :].astype(BF16)), *[send_x(far[d].astype(BF16), d) for d in (1, 2, 3)]
    )
    near = near[: rows // 2] + n1.astype(F32)
    far = far[0] + f1.astype(F32) + f2.astype(F32) + f3.astype(F32)
    both = jnp.concatenate([near, far], 1).reshape(NZ // 2, half, 2 * width)
    total = both[0]
    for v in together(*[send_z(both[k].astype(BF16), 2 * k) for k in (1, 2, 3)]):
        total = total + v.astype(F32)
    total = total.astype(BF16)
    mine, other = total[:, :width], core(total[:, width:])
    return jnp.where(c == 0, jnp.concatenate([mine, other], 0), jnp.concatenate([other, mine], 0))


def solution(mesh):
    placed = (
        P("wide", "narrow"),
        P("narrow", "wide"),
        P("narrow", "wide"),
        P("wide", "narrow"),
        P("narrow", "wide", None),
        P("narrow", None, "wide"),
        P(),
    )
    return jax.shard_map(body, mesh=mesh, in_specs=placed, out_specs=P("wide", "narrow"), check_vma=False)
```

```python
import functools

import jax
import jax.numpy as jnp
from jax import lax
from jax.experimental import pallas as pl
from jax.experimental.pallas import tpu as pltpu
from jax.sharding import PartitionSpec as P

NX, NZ, NY, NC = 4, 8, 4, 2
F32, BF16 = jnp.float32, jnp.bfloat16
MIB = 1024 * 1024


def device(x, z, y, c):
    return (x % NX * NZ + z % NZ) * NY * NC + y % NY * NC + c


def send_x(v, d):
    return lax.ppermute(v, "wide", [(x * NZ + z, (x + d) % NX * NZ + z) for x in range(NX) for z in range(NZ)])


def send_z(v, d):
    return lax.ppermute(v, "wide", [(x * NZ + z, x * NZ + (z + d) % NZ) for x in range(NX) for z in range(NZ)])


def send_y(v, d):
    return lax.ppermute(v, "narrow", [(y * NC + c, (y + d) % NY * NC + c) for y in range(NY) for c in range(NC)])


def send_pair(v):
    return lax.ppermute(v, "wide", [(i, i ^ 1) for i in range(NX * NZ)])


def core(v):
    return lax.ppermute(v, "narrow", [(i, i ^ 1) for i in range(NY * NC)])


HOME_GROUPS = [
    [device(x, z + p, y, c) for x in range(NX) for y in range(NY) for p in range(2)]
    for z in range(0, NZ, 2)
    for c in range(NC)
]


def dot(a, b):
    return jnp.dot(a, b, preferred_element_type=F32)


SMEM = pl.BlockSpec(memory_space=pltpu.SMEM)
VMEM = pl.BlockSpec(memory_space=pltpu.VMEM)
HBM = pl.BlockSpec(memory_space=pltpu.HBM)


def params(limit=60 * MIB):
    return pltpu.CompilerParams(vmem_limit_bytes=limit)


def together(*v):
    return lax.optimization_barrier(v)


def in_hbm(*arrays):
    return [pltpu.with_memory_space_constraint(v, pltpu.HBM) for v in arrays]


def pick_kernel(place, q0, q1, q2, q3, keep, give):
    c = place[3]
    half = q0.shape[0] // 2
    for k, ref in enumerate((q0, q1, q2, q3)):
        at = slice(k * half, (k + 1) * half)
        keep[at, :] = ref[pl.ds(pl.multiple_of(c * half, half), half), :]
        give[at, :] = ref[pl.ds(pl.multiple_of((1 - c) * half, half), half), :]


def join_kernel(n0, n1, f0, f1, f2, f3, near, far):
    some = n0.shape[0]
    for k, ref in enumerate((n0, n1)):
        near[k * some : (k + 1) * some, :] = ref[...]
    for k, ref in enumerate((f0, f1, f2, f3)):
        far[k * some : (k + 1) * some, :] = ref[...]


def shrink_kernel(own, rank, place, index, p0, p1, p2, p3, q0, q1, a_n, a_f, t, low):
    x, z, first = place[0], place[1], place[4]
    half = t.shape[0] // (NX * NZ)
    width = a_n.shape[0]
    quads = NZ // 2

    def put(ref, at, dx, pair, k, columns):
        from_z = ((z ^ pair) + 2 * k) % NZ
        row = pl.multiple_of(((x + dx) % NX * NZ + from_z) * half, half)
        t[pl.ds(row, half), columns] = ref[at * half : (at + 1) * half, :]

    for dx, ref in enumerate((p0, p1, p2, p3)):
        for pair in range(2):
            for k in range(quads):
                put(ref, pair * quads + k, dx, pair, k, slice(0, width))
    for pair, ref in enumerate((q0, q1)):
        for dx in range(NX):
            for k in range(quads):
                put(ref, dx * quads + k, dx, pair, k, slice(width, 2 * width))
    s = dot(t[:, :width], a_n[...]) + dot(t[:, width:], a_f[...])
    total = jnp.zeros((t.shape[0], rank), F32)
    for k in range(own):
        total = jnp.where(index[...] == first + k, s[:, k * rank : (k + 1) * rank], total)
    some = NZ * half // 4
    total = total.reshape(NX, 2, 2 * some, rank)
    total = jnp.concatenate([total[:, :, :some], total[:, :, some:]], 3)
    for b in range(NX):
        for y in range(NY):
            for p in range(2):
                low[(b * NY + y) * 2 + p] = total[b, p]


def gate_kernel(place, t, w_n, w_f, mine, o1, o2, o3):
    y = place[2]
    rows, width = mine.shape[0], w_n.shape[0]
    for e, ref in enumerate((mine, o1, o2, o3)):
        at = pl.ds(pl.multiple_of((y + e) % NY * rows, rows), rows)
        part = dot(t[at, :width], w_n[...]) + dot(t[at, width:], w_f[...])
        ref[...] = part.astype(ref.dtype)


def base_kernel(t, w_n, w_f, up, v_t, v_n, v_f, v_up, sems):
    width, rows = w_n.shape[0], t.shape[0] // 2
    get = [
        pltpu.make_async_copy(t.at[:, :width], v_t.at[:, :width], sems.at[0]),
        pltpu.make_async_copy(w_n, v_n, sems.at[1]),
        pltpu.make_async_copy(t.at[:, width:], v_t.at[:, width:], sems.at[2]),
        pltpu.make_async_copy(w_f, v_f, sems.at[3]),
    ]
    for copy in get:
        copy.start()
    get[0].wait()
    get[1].wait()
    for i in range(2):
        at = pl.ds(i * rows, rows)
        v_up[at, :] = dot(v_t[at, :width], v_n[...])
    get[2].wait()
    get[3].wait()
    put = []
    for i in range(2):
        at = pl.ds(i * rows, rows)
        v_up[at, :] += dot(v_t[at, width:], v_f[...])
        put.append(pltpu.make_async_copy(v_up.at[at, :], up.at[at, :], sems.at[4 + i]))
        put[-1].start()
    for copy in put:
        copy.wait()


def up_kernel(rank, place, index, low, up, b_n, b_f, mine, o1, o2, o3, total, wide_low):
    k, y = pl.program_id(0), place[2]
    step = b_n.shape[0]
    count = step // rank
    rows = mine.shape[0]

    @pl.when(k == 0)
    def _():
        v = jnp.sum(low[...].astype(F32).reshape(NX, NZ // 2, 2, rows // 4, 2 * rank), 1)
        v = jnp.concatenate([v[:, :, :, :rank], v[:, :, :, rank:]], 2).reshape(NX * rows, rank)
        wide_low[...] = jnp.concatenate([v] * count, 1)
        total[...] = up[...]

    group = (lax.broadcasted_iota(jnp.int32, (NX * rows, step), 1) >> (rank.bit_length() - 1)) + k * count
    own = index[...] - place[5]
    far = index[...] - place[6]
    spread_n = jnp.where(own == group, wide_low[...], 0.0).astype(BF16)
    spread_f = jnp.where(far == group, wide_low[...], 0.0).astype(BF16)
    total[...] += dot(spread_n, b_n[...]) + dot(spread_f, b_f[...])

    @pl.when(k == pl.num_programs(0) - 1)
    def _():
        for e, ref in enumerate((mine, o1, o2, o3)):
            at = pl.ds(pl.multiple_of((y + e) % NY * rows, rows), rows)
            ref[...] = total[at, :].astype(ref.dtype)


def mix_kernel(place, h0, h1, h2, h3, d_n, d_f, near0, near1, near2, near3, far0, far1, h):
    x, z, y = place[0], place[1], place[2]
    half = h0.shape[0] // NZ
    quads = NZ // 2
    for e, ref in enumerate((h0, h1, h2, h3)):
        dx = (y + e - x + NX) % NX
        for pair in range(2):
            for k in range(quads):
                to_z = ((z ^ pair) + 2 * k) % NZ
                to = pl.multiple_of(((dx * 2 + pair) * quads + k) * half, half)
                h[pl.ds(to, half), :] = ref[pl.ds(pl.multiple_of(to_z * half, half), half), :]
    rows = NZ * half
    near = dot(h[...], d_n[...])
    for dx, ref in enumerate((near0, near1, near2, near3)):
        ref[...] = near[dx * rows : (dx + 1) * rows].astype(ref.dtype)
    far = dot(h[...], d_f[...])
    some = rows // 2
    for dx in range(NX):
        for pair, ref in enumerate((far0, far1)):
            at = (dx * 2 + pair) * some
            ref[dx * some : (dx + 1) * some, :] = far[at : at + some].astype(ref.dtype)


def body(tokens, gate, up, down, a, b, index):
    w, n = lax.axis_index("wide"), lax.axis_index("narrow")
    x, z, y, c = w // NZ, w % NZ, n // NC, n % NC
    width, hid = gate.shape
    own_a, rank, own_b = a.shape[1], a.shape[2], b.shape[0]
    half = tokens.shape[0] // 2
    rows = NZ * half
    everyone = NX * rows
    shape = jax.ShapeDtypeStruct

    b_n = b.reshape(own_b * rank, hid)
    place = jnp.stack([x, z, y, c, w * own_a, n * own_b, (n ^ 1) * own_b]).astype(jnp.int32)
    column = lax.dynamic_index_in_dim(index.reshape(NX * NZ, 2, half), c, 1, keepdims=False).reshape(everyone, 1)

    *quad, b_f, gate_f, place, column = together(
        *[send_z(tokens, -2 * k) for k in (1, 2, 3)], core(b_n), core(gate), place, column
    )
    near, far = pl.pallas_call(
        pick_kernel,
        out_shape=(shape((rows // 2, width), BF16),) * 2,
        in_specs=[SMEM] + [VMEM] * 4,
        out_specs=(VMEM,) * 2,
        compiler_params=params(4 * MIB),
        name="pick",
    )(place, *in_hbm(tokens), *quad)
    far, up = together(core(far), up)
    a_n = a.reshape(width, own_a * rank)
    pair, *fars, a_f = together(send_pair(near), *[send_x(far, -d) for d in (1, 2, 3)], core(a_n))
    near, far = pl.pallas_call(
        join_kernel,
        out_shape=(shape((rows, width), BF16), shape((everyone // 2, width), BF16)),
        in_specs=[VMEM] * 6,
        out_specs=(VMEM,) * 2,
        compiler_params=params(4 * MIB),
        name="join",
    )(near, pair, far, *fars)
    *pieces, up_f = together(near, *[send_x(near, -d) for d in (1, 2, 3)], far, send_pair(far), core(up))
    down, gate = together(down, gate, up_f)[:2]
    down_f = core(down)
    t, low = pl.pallas_call(
        functools.partial(shrink_kernel, own_a, rank),
        out_shape=(shape((everyone, 2 * width), BF16),) + (shape((2 * NX * NY, rows // 4, 2 * rank), F32),),
        in_specs=[SMEM] + [VMEM] * 9,
        out_specs=(VMEM,) * 2,
        compiler_params=params(),
        name="shrink",
    )(place, column, *pieces, a_n, a_f)

    blocks = (shape((rows, hid), F32),) + (shape((rows, hid), BF16),) * 3

    def reduce_y(mine, *others):
        for e, part in enumerate(others, 1):
            mine = mine + send_y(part, e).astype(F32)
        return mine

    gates = pl.pallas_call(
        gate_kernel,
        out_shape=blocks,
        in_specs=[SMEM] + [VMEM] * 3,
        out_specs=(VMEM,) * 4,
        compiler_params=params(),
        name="gate",
    )(place, t, gate, gate_f)

    low, t, *gates = together(
        lax.all_to_all(low, ("wide", "narrow"), 0, 0, tiled=True, axis_index_groups=HOME_GROUPS), t, *gates
    )
    low = lax.dynamic_slice_in_dim(low, y * 2 * NY, 2 * NY, 0)
    low = jnp.sum(low, 0).astype(BF16)
    low = lax.all_to_all(jnp.broadcast_to(low, (NX * NZ,) + low.shape), "wide", 0, 0, tiled=True)

    up_part = pl.pallas_call(
        base_kernel,
        out_shape=shape((everyone, hid), F32),
        in_specs=[HBM] * 3,
        out_specs=HBM,
        scratch_shapes=[
            pltpu.VMEM((everyone, 2 * width), BF16),
            pltpu.VMEM((width, hid), BF16),
            pltpu.VMEM((width, hid), BF16),
            pltpu.VMEM((everyone, hid), F32),
            pltpu.SemaphoreType.DMA((6,)),
        ],
        compiler_params=params(),
        name="base",
    )(t, up, up_f)
    gate_sum = reduce_y(*gates)
    steps = 4
    part = pl.BlockSpec((own_b * rank // steps, hid), lambda k: (k, 0))
    fixed = lambda *dims: pl.BlockSpec(dims, lambda k: (0,) * len(dims))
    up_sum = reduce_y(
        *pl.pallas_call(
            functools.partial(up_kernel, rank),
            out_shape=blocks,
            grid=(steps,),
            in_specs=[SMEM, fixed(everyone, 1), fixed(*low.shape), fixed(everyone, hid), part, part],
            out_specs=(fixed(rows, hid),) * 4,
            scratch_shapes=[pltpu.VMEM((everyone, hid), F32), pltpu.VMEM((everyone, own_b * rank // steps), F32)],
            compiler_params=params(32 * MIB),
            name="up",
        )(place, column, low, *in_hbm(up_part, b_n, b_f))
    )
    hidden = (jax.nn.silu(gate_sum) * up_sum).astype(BF16)

    some = everyone // 2
    near, n1, n2, n3, far, f1 = pl.pallas_call(
        mix_kernel,
        out_shape=(shape((rows, width), F32),)
        + (shape((rows, width), BF16),) * 3
        + (shape((some, width), F32), shape((some, width), BF16)),
        in_specs=[SMEM] + [VMEM] * 6,
        out_specs=(VMEM,) * 6,
        scratch_shapes=[pltpu.VMEM((everyone, hid), BF16)],
        compiler_params=params(24 * MIB),
        name="mix",
    )(place, hidden, *[send_y(hidden, -e) for e in (1, 2, 3)], down, down_f)
    n1, n2, n3, f1 = together(send_x(n1, 1), send_x(n2, 2), send_x(n3, 3), send_pair(f1))
    near = near + n1.astype(F32) + n2.astype(F32) + n3.astype(F32)
    far = (far + f1.astype(F32)).reshape(NX, rows // 2, width)
    n1, f1, f2, f3 = together(
        send_pair(near[rows // 2 :].astype(BF16)), *[send_x(far[d].astype(BF16), d) for d in (1, 2, 3)]
    )
    near = near[: rows // 2] + n1.astype(F32)
    far = far[0] + f1.astype(F32) + f2.astype(F32) + f3.astype(F32)
    both = jnp.concatenate([near, far], 1).reshape(NZ // 2, half, 2 * width)
    total = both[0]
    for v in together(*[send_z(both[k].astype(BF16), 2 * k) for k in (1, 2, 3)]):
        total = total + v.astype(F32)
    total = total.astype(BF16)
    mine, other = total[:, :width], core(total[:, width:])
    return jnp.where(c == 0, jnp.concatenate([mine, other], 0), jnp.concatenate([other, mine], 0))


def solution(mesh):
    placed = (
        P("wide", "narrow"),
        P("narrow", "wide"),
        P("narrow", "wide"),
        P("wide", "narrow"),
        P("narrow", "wide", None),
        P("narrow", None, "wide"),
        P(),
    )
    return jax.shard_map(body, mesh=mesh, in_specs=placed, out_specs=P("wide", "narrow"), check_vma=False)
```
